32 devices in a mesh: parts: 2 (over x), shift: 16 (over z, y, core).
Axes of the slice: x: 2, y: 2, z: 4, core: 2. Of those that a mesh axis runs over, the one named last changes fastest.
Arguments:
- embeddings: bfloat16 [16384, 768], P(('parts', 'shift')), parts along dimension 0, as said below
- block_cluster: int32 [128], P(('parts', 'shift')), parts along dimension 0, may hold values from 0 to 7, never falling along the last dimension, each value on 1 to 16 neighbouring positions
Outputs:
- best_match: float32 [16384], P(('parts', 'shift')), parts along dimension 0
The draws below stay inside these ranges and needn't reach their ends.
There are 2 independent parts, one for each index of `parts`. The reference program is written for one: setup_inputs(seed, part) draws one part's arguments, and reference() takes and returns one part's arrays. A program takes and returns all parts, laid end to end along the dimension named above; each array names one. Nothing has to cross between parts.
Inputs may be any that keep to these rules, and one draw needn't show every extreme that they name: block_cluster never falls along the blocks; each cluster holds 1 to 16 consecutive blocks and one holds exactly 16. `embeddings`: every row is nonzero; rows may differ in scale, which the first step removes.
All inputs are finite; a program needn't handle non-finite values.
Results may differ from the reference program's by a relative error of at most 0.00059.
Values may be sent and summed in bfloat16 or wider, within the bound.
No kernel may reach another device: no remote copies, remote signals or barrier semaphores. Data moves between devices by JAX's collectives and lax.ppermute only.
A program may use at most 64 MiB of HBM per device.

```python
import math
import jax
import jax.numpy as jnp
import numpy as np
from jax import lax

D = 768
BLK = 128
MOST_BLK = 16
ROWS_DEV = 512
ROWS = 8192
NBLK = 64
NCLUST = 8


def draw_embeddings(key, part):
    key = jax.random.fold_in(key, 11)
    keys = jax.random.split(key, 4)
    base = jax.random.normal(keys[0], (ROWS, D), jnp.float32)
    offsets = jax.random.randint(keys[1], (ROWS,), 1, 3 * ROWS_DEV + 1)
    partner = (jnp.arange(ROWS, dtype=jnp.int32) - offsets) % ROWS
    copied = base[partner]
    weight = jax.random.uniform(keys[2], (ROWS, 1), jnp.float32, 0.3, 0.95)
    chosen = jax.random.bernoulli(keys[3], 0.5, (ROWS, 1))
    share = jnp.where(chosen, weight, 0.0)
    mixed = share * copied + jnp.sqrt(1.0 - share * share) * base
    return mixed.astype(jnp.bfloat16)


def length_profile(number_of, total, limit, skew):
    weights = [(1 << 20) // math.isqrt(rank ** skew) + 1 for rank in range(2, number_of + 1)]
    surplus, counts = total - limit - (number_of - 1), [1] * (number_of - 1)
    while surplus > 0:
        movable = [i for i in range(number_of - 1) if counts[i] < limit]
        whole, left = sum([weights[i] for i in movable]), surplus
        for i in movable:
            more = min(limit - counts[i], max(1, left * weights[i] // whole), surplus)
            counts[i] = counts[i] + more
            surplus = surplus - more
    return np.array([limit] + counts)


def ragged(own_key, amount, total, reach, lean):
    if amount == 2:
        one = jax.random.randint(own_key, (), max(1, total - reach), min(reach, total - 1) + 1)
        return jnp.stack([one, total - one])
    tallies = jnp.asarray(length_profile(amount, total, reach, lean), jnp.int32)
    pairs = (amount - 1) // 2
    giver, taker = tallies[1:1 + 2 * pairs:2], tallies[2:2 + 2 * pairs:2]
    slack = jnp.minimum(giver - 1, reach - taker)
    moved = jax.random.randint(jax.random.fold_in(own_key, 1), (pairs,), 0, 1 << 20) % (slack + 1)
    tallies = tallies.at[1:1 + 2 * pairs:2].set(giver - moved).at[2:2 + 2 * pairs:2].set(taker + moved)
    return tallies[jax.random.permutation(jax.random.fold_in(own_key, 2), amount)]


def setup_inputs(seed: int = 0, part: int = 0) -> dict:
    streams_of = jax.random.split(jax.random.key(seed), 3)
    own_keys = jax.random.split(jax.random.fold_in(streams_of[2], part), 3)
    embeddings = draw_embeddings(jax.random.fold_in(jax.random.fold_in(streams_of[2], part), 71), part)
    block_cluster = jnp.searchsorted(jnp.cumsum(ragged(own_keys[1], NCLUST, NBLK, MOST_BLK, 2)), jnp.arange(NBLK), side="right").astype(jnp.int32)
    return dict(embeddings=embeddings, block_cluster=block_cluster)


def reference(embeddings, block_cluster):
    values = embeddings.astype(jnp.float32)
    scale = lax.rsqrt(lax.optimization_barrier(jnp.mean(values * values, axis=1, keepdims=True)) + 1e-06) / math.sqrt(embeddings.shape[1])
    unit = (values * scale).astype(jnp.bfloat16)
    cluster = jnp.repeat(block_cluster, BLK)
    total = unit.shape[0]
    index = jnp.arange(total, dtype=jnp.int32)
    pieces = total // ROWS_DEV

    def one_block(args):
        rows_unit, rows_cluster, rows_index = args
        sims = jnp.dot(rows_unit, unit.T, preferred_element_type=jnp.float32)
        mask = (rows_cluster[:, None] == cluster[None, :]) & (rows_index[:, None] != index[None, :])
        top = lax.optimization_barrier(jnp.max(jnp.where(mask, sims, jnp.float32(-2.0)), axis=1))
        return jnp.maximum(top, jnp.float32(-1.0))
    result = lax.map(one_block, (unit.reshape(pieces, ROWS_DEV, unit.shape[1]), cluster.reshape(pieces, ROWS_DEV), index.reshape(pieces, ROWS_DEV)))
    return result.reshape(total)
```

```python
import functools
import math

import jax
import jax.numpy as jnp
from jax import lax
from jax.experimental import pallas as pl
from jax.experimental.pallas import tpu as pltpu
from jax.sharding import PartitionSpec as P

LOW = -2.0
QUAD = 4


def swapped(array, mask):
    length = lax.axis_size("shift")
    return lax.ppermute(array, "shift", [(i, i ^ mask) for i in range(length)])


def moved(array, by):
    length = lax.axis_size("shift")
    pairs = [(i, i + by) for i in range(length) if 0 <= i + by < length]
    return lax.ppermute(array, "shift", pairs)


def unit_rows(raw):
    values = raw.astype(jnp.float32)
    scale = lax.rsqrt(jnp.mean(values * values, axis=1, keepdims=True) + 1e-06) / math.sqrt(
        raw.shape[1]
    )
    return (values * scale).astype(jnp.bfloat16)


def product(rows, columns):
    return lax.dot_general(
        rows, columns, (((1,), (1,)), ((), ())), preferred_element_type=jnp.float32
    )


def shares(ids, p, q, blocks):
    hit = ids[p, 0] == ids[q, 0]
    for a in range(blocks):
        for b in range(blocks):
            hit = jnp.logical_or(hit, ids[p, a] == ids[q, b])
    return hit


def column_best(ids, p, q, sims, blocks, width, own=False):
    pieces = []
    for b in range(blocks):
        top = jnp.full((8, width), LOW, jnp.float32)
        for a in range(blocks):
            tile = sims[a * width : (a + 1) * width, b * width : (b + 1) * width]
            if own and a == b:
                same = lax.broadcasted_iota(jnp.int32, (width, width), 0) == (
                    lax.broadcasted_iota(jnp.int32, (width, width), 1)
                )
                tile = jnp.where(same, LOW, tile)
            part = jnp.max(tile.reshape(width // 8, 8, width), axis=0)
            top = jnp.maximum(top, jnp.where(ids[p, a] == ids[q, b], part, LOW))
        pieces.append(jnp.max(top, axis=0, keepdims=True))
    return jnp.concatenate(pieces, axis=1)


def row_best(ids, p, q, sims, blocks, width):
    pieces = []
    for a in range(blocks):
        top = jnp.full((width, width), LOW, jnp.float32)
        for b in range(blocks):
            tile = sims[a * width : (a + 1) * width, b * width : (b + 1) * width]
            top = jnp.maximum(top, jnp.where(ids[p, a] == ids[q, b], tile, LOW))
        pieces.append(jnp.max(top.T, axis=0, keepdims=True))
    return jnp.concatenate(pieces, axis=1)


def near_kernel(blocks, ids, own_ref, mate_ref, own_unit, mate_unit, best):
    rows = own_ref.shape[0]
    width = rows // blocks
    own_unit[...] = unit_rows(own_ref[...])
    mate_unit[...] = unit_rows(mate_ref[...])
    sims = product(own_unit[...], own_unit[...])
    best[...] = column_best(ids, 0, 0, sims, blocks, width, own=True)

    @pl.when(shares(ids, 1, 0, blocks))
    def _():
        sims = product(mate_unit[...], own_unit[...])
        best[...] = jnp.maximum(best[...], column_best(ids, 1, 0, sims, blocks, width))


def partner_kernel(blocks, ids, own_unit, partner_ref, best_in, partner_unit, best):
    rows = own_unit.shape[0]
    width = rows // blocks
    partner_unit[...] = unit_rows(partner_ref[...])
    best[...] = best_in[...]

    @pl.when(shares(ids, 2, 0, blocks))
    def _():
        sims = product(partner_unit[...], own_unit[...])
        best[...] = jnp.maximum(best[...], column_best(ids, 2, 0, sims, blocks, width))


def far_kernel(
    blocks, ids, own_unit, mate_unit, partner_unit, cross_ref, back_ref, best_in,
    best, far, back, cross_unit, back_unit,
):
    rows = own_unit.shape[0]
    width = rows // blocks
    cross_unit[...] = unit_rows(cross_ref[...])
    back_unit[...] = unit_rows(back_ref[...])
    best[...] = best_in[...]
    back[...] = jnp.full_like(back, LOW)
    far[...] = jnp.full_like(far, LOW)

    @pl.when(shares(ids, 3, 0, blocks))
    def _():
        sims = product(cross_unit[...], own_unit[...])
        best[...] = jnp.maximum(best[...], column_best(ids, 3, 0, sims, blocks, width))

    for q, held in enumerate((own_unit, mate_unit, partner_unit, cross_unit)):

        @pl.when(shares(ids, q, 4, blocks))
        def _(q=q, held=held):
            sims = product(held[...], back_unit[...])
            back[...] = jnp.maximum(back[...], column_best(ids, q, 4, sims, blocks, width))
            mine = row_best(ids, q, 4, sims, blocks, width)
            if q == 0:
                best[...] = jnp.maximum(best[...], mine)
            else:
                far[q - 1 : q, :] = mine


def local(embeddings, block_cluster):
    rows, depth = embeddings.shape
    blocks = block_cluster.shape[0]
    count = lax.axis_size("shift")
    mine = lax.axis_index("shift")

    partner_raw = swapped(embeddings, 2)
    back_raw = moved(embeddings, QUAD)
    mate_raw = swapped(embeddings, 1)
    own_ids = block_cluster + 1
    ids = jnp.stack(
        [
            own_ids,
            swapped(own_ids, 1),
            swapped(own_ids, 2),
            swapped(own_ids, 3),
            moved(own_ids, QUAD),
        ]
    )

    smem = pl.BlockSpec(memory_space=pltpu.SMEM)
    vmem = pl.BlockSpec(memory_space=pltpu.VMEM)
    units = jax.ShapeDtypeStruct((rows, depth), jnp.bfloat16)
    line = jax.ShapeDtypeStruct((1, rows), jnp.float32)
    params = pltpu.CompilerParams(vmem_limit_bytes=48 * 1024 * 1024)
    flops = 2 * rows * rows * depth

    own_unit, mate_unit, best = pl.pallas_call(
        functools.partial(near_kernel, blocks),
        out_shape=(units, units, line),
        in_specs=[smem, vmem, vmem],
        out_specs=(vmem, vmem, vmem),
        compiler_params=params,
        cost_estimate=pl.CostEstimate(flops=2 * flops, bytes_accessed=8 * rows * depth, transcendentals=0),
    )(ids, embeddings, mate_raw)

    cross_raw = swapped(partner_raw, 1)
    partner_unit, best = pl.pallas_call(
        functools.partial(partner_kernel, blocks),
        out_shape=(units, line),
        in_specs=[smem, vmem, vmem, vmem],
        out_specs=(vmem, vmem),
        compiler_params=params,
        cost_estimate=pl.CostEstimate(flops=flops, bytes_accessed=6 * rows * depth, transcendentals=0),
    )(ids, own_unit, partner_raw, best)

    best, far, back = pl.pallas_call(
        functools.partial(far_kernel, blocks),
        out_shape=(line, jax.ShapeDtypeStruct((3, rows), jnp.float32), line),
        in_specs=[smem] + [vmem] * 6,
        out_specs=(vmem, vmem, vmem),
        scratch_shapes=[
            pltpu.VMEM((rows, depth), jnp.bfloat16),
            pltpu.VMEM((rows, depth), jnp.bfloat16),
        ],
        compiler_params=params,
        cost_estimate=pl.CostEstimate(flops=5 * flops, bytes_accessed=10 * rows * depth, transcendentals=0),
    )(ids, own_unit, mate_unit, partner_unit, cross_raw, back_raw, best)

    from_next = moved(back, -QUAD)
    from_next = jnp.where(mine + QUAD < count, from_next, LOW)
    from_mate = swapped(jnp.concatenate([far[0:1], far[2:3]]), 1)
    from_partner = swapped(jnp.maximum(far[1:2], from_mate[1:2]), 2)
    best = jnp.maximum(jnp.maximum(best, from_next), jnp.maximum(from_mate[0:1], from_partner))
    return jnp.maximum(best.reshape(rows), -1.0)


def solution(mesh):
    return jax.shard_map(
        local,
        mesh=mesh,
        in_specs=(P(("parts", "shift"), None), P(("parts", "shift"))),
        out_specs=P(("parts", "shift")),
        check_vma=False,
    )
```

```python
import functools
import math

import jax
import jax.numpy as jnp
from jax import lax
from jax.experimental import pallas as pl
from jax.experimental.pallas import tpu as pltpu
from jax.sharding import PartitionSpec as P

LOW = -2.0
QUAD = 4


def swapped(array, mask):
    length = lax.axis_size("shift")
    return lax.ppermute(array, "shift", [(i, i ^ mask) for i in range(length)])


def next_quad():
    parts, count = lax.axis_size("parts"), lax.axis_size("shift")
    pairs = []
    for part in range(parts):
        by = QUAD if part % 2 == 0 else -QUAD
        for i in range(count):
            there = i + by
            if 0 <= there < count:
                pairs.append((part * count + i, part * count + there))
            elif part ^ 1 < parts:
                pairs.append((part * count + i, (part ^ 1) * count + i))
    return pairs


def forward(array):
    return lax.ppermute(array, ("parts", "shift"), next_quad())


def backward(array):
    return lax.ppermute(array, ("parts", "shift"), [(b, a) for a, b in next_quad()])


def unit_rows(raw):
    values = raw.astype(jnp.float32)
    scale = lax.rsqrt(jnp.mean(values * values, axis=1, keepdims=True) + 1e-06) / math.sqrt(
        raw.shape[1]
    )
    return (values * scale).astype(jnp.bfloat16)


def product(rows, columns):
    return lax.dot_general(
        rows, columns, (((1,), (1,)), ((), ())), preferred_element_type=jnp.float32
    )


def shares(ids, p, q, blocks):
    hit = ids[p, 0] == ids[q, 0]
    for a in range(blocks):
        for b in range(blocks):
            hit = jnp.logical_or(hit, ids[p, a] == ids[q, b])
    return hit


def column_best(ids, p, q, sims, blocks, width, own=False):
    pieces = []
    for b in range(blocks):
        top = jnp.full((8, width), LOW, jnp.float32)
        for a in range(blocks):
            tile = sims[a * width : (a + 1) * width, b * width : (b + 1) * width]
            if own and a == b:
                same = lax.broadcasted_iota(jnp.int32, (width, width), 0) == (
                    lax.broadcasted_iota(jnp.int32, (width, width), 1)
                )
                tile = jnp.where(same, LOW, tile)
            part = jnp.max(tile.reshape(width // 8, 8, width), axis=0)
            top = jnp.maximum(top, jnp.where(ids[p, a] == ids[q, b], part, LOW))
        pieces.append(jnp.max(top, axis=0, keepdims=True))
    return jnp.concatenate(pieces, axis=1)


def row_best(ids, p, q, sims, blocks, width):
    pieces = []
    for a in range(blocks):
        top = jnp.full((width, width), LOW, jnp.float32)
        for b in range(blocks):
            tile = sims[a * width : (a + 1) * width, b * width : (b + 1) * width]
            top = jnp.maximum(top, jnp.where(ids[p, a] == ids[q, b], tile, LOW))
        pieces.append(jnp.max(top.T, axis=0, keepdims=True))
    return jnp.concatenate(pieces, axis=1)


def near_kernel(blocks, ids, own_ref, mate_ref, own_unit, mate_unit, best):
    rows = own_ref.shape[0]
    width = rows // blocks
    own_unit[...] = unit_rows(own_ref[...])
    mate_unit[...] = unit_rows(mate_ref[...])
    sims = product(own_unit[...], own_unit[...])
    best[...] = column_best(ids, 0, 0, sims, blocks, width, own=True)

    @pl.when(shares(ids, 1, 0, blocks))
    def _():
        sims = product(mate_unit[...], own_unit[...])
        best[...] = jnp.maximum(best[...], column_best(ids, 1, 0, sims, blocks, width))


def partner_kernel(blocks, ids, own_unit, partner_ref, best_in, partner_unit, best):
    rows = own_unit.shape[0]
    width = rows // blocks
    partner_unit[...] = unit_rows(partner_ref[...])
    best[...] = best_in[...]

    @pl.when(shares(ids, 2, 0, blocks))
    def _():
        sims = product(partner_unit[...], own_unit[...])
        best[...] = jnp.maximum(best[...], column_best(ids, 2, 0, sims, blocks, width))


def first_kernel(
    blocks, ids, own_unit, mate_unit, cross_ref, back_ref, best_in,
    best, to_mate, back, back_unit, cross_unit,
):
    rows = own_unit.shape[0]
    width = rows // blocks
    cross_unit[...] = unit_rows(cross_ref[...])
    back_unit[...] = unit_rows(back_ref[...])
    best[...] = best_in[...]
    back[...] = jnp.full_like(back, LOW)
    to_mate[...] = jnp.full_like(to_mate, LOW)

    for row, (q, held) in enumerate(((1, mate_unit), (3, cross_unit))):

        @pl.when(shares(ids, q, 4, blocks))
        def _(row=row, q=q, held=held):
            sims = product(held[...], back_unit[...])
            back[...] = jnp.maximum(back[...], column_best(ids, q, 4, sims, blocks, width))
            to_mate[row : row + 1, :] = row_best(ids, q, 4, sims, blocks, width)

    @pl.when(shares(ids, 3, 0, blocks))
    def _():
        sims = product(cross_unit[...], own_unit[...])
        best[...] = jnp.maximum(best[...], column_best(ids, 3, 0, sims, blocks, width))


def second_kernel(
    blocks, ids, own_unit, partner_unit, back_unit, best_in, back_in,
    best, to_partner, back,
):
    rows = own_unit.shape[0]
    width = rows // blocks
    best[...] = best_in[...]
    back[...] = back_in[...]
    to_partner[...] = jnp.full_like(to_partner, LOW)

    for q, held in ((0, own_unit), (2, partner_unit)):

        @pl.when(shares(ids, q, 4, blocks))
        def _(q=q, held=held):
            sims = product(held[...], back_unit[...])
            back[...] = jnp.maximum(back[...], column_best(ids, q, 4, sims, blocks, width))
            mine = row_best(ids, q, 4, sims, blocks, width)
            if q == 0:
                best[...] = jnp.maximum(best[...], mine)
            else:
                to_partner[...] = mine


def local(embeddings, block_cluster):
    rows, depth = embeddings.shape
    blocks = block_cluster.shape[0]
    count = lax.axis_size("shift")
    mine = lax.axis_index("shift")
    upward = lax.axis_index("parts") % 2 == 0
    has_quad_below = mine >= QUAD
    has_quad_above = mine + QUAD < count
    receives = jnp.where(upward, has_quad_below, has_quad_above)
    returns = jnp.where(upward, has_quad_above, has_quad_below)

    partner_raw = swapped(embeddings, 2)
    back_raw = forward(embeddings)
    mate_raw = swapped(embeddings, 1)
    mate_raw, block_cluster = lax.optimization_barrier((mate_raw, block_cluster))
    ids = jnp.stack(
        [
            block_cluster,
            swapped(block_cluster, 1),
            swapped(block_cluster, 2),
            swapped(block_cluster, 3),
            jnp.where(receives, forward(block_cluster), -1),
        ]
    )

    smem = pl.BlockSpec(memory_space=pltpu.SMEM)
    vmem = pl.BlockSpec(memory_space=pltpu.VMEM)
    units = jax.ShapeDtypeStruct((rows, depth), jnp.bfloat16)
    line = jax.ShapeDtypeStruct((1, rows), jnp.float32)
    lines = jax.ShapeDtypeStruct((2, rows), jnp.float32)
    flops = 2 * rows * rows * depth

    def call(kernel, products, outs, inputs, scratch=()):
        return pl.pallas_call(
            functools.partial(kernel, blocks),
            out_shape=outs,
            in_specs=[smem] + [vmem] * len(inputs),
            out_specs=(vmem,) * len(outs),
            scratch_shapes=scratch,
            compiler_params=pltpu.CompilerParams(vmem_limit_bytes=48 * 1024 * 1024),
            cost_estimate=pl.CostEstimate(
                flops=products * flops, bytes_accessed=2 * rows * depth, transcendentals=0
            ),
        )(ids, *inputs)

    own_unit, mate_unit, best = call(
        near_kernel, 0, (units, units, line), (embeddings, mate_raw)
    )
    partner_raw, best = lax.optimization_barrier((partner_raw, best))
    cross_raw = swapped(partner_raw, 1)
    partner_unit, best = call(
        partner_kernel, 0, (units, line), (own_unit, partner_raw, best)
    )
    best, to_mate, back, back_unit = call(
        first_kernel, 3, (line, lines, line, units),
        (own_unit, mate_unit, cross_raw, back_raw, best),
        (pltpu.VMEM((rows, depth), jnp.bfloat16),),
    )
    from_mate = swapped(to_mate, 1)
    best, to_partner, back = call(
        second_kernel, 2, (line, line, line), (own_unit, partner_unit, back_unit, best, back)
    )
    from_next = jnp.where(returns, backward(back), LOW)
    from_partner = swapped(jnp.maximum(to_partner, from_mate[1:2]), 2)
    best = jnp.maximum(jnp.maximum(best, from_next), jnp.maximum(from_mate[0:1], from_partner))
    return jnp.maximum(best.reshape(rows), -1.0)


def solution(mesh):
    return jax.shard_map(
        local,
        mesh=mesh,
        in_specs=(P(("parts", "shift"), None), P(("parts", "shift"))),
        out_specs=P(("parts", "shift")),
        check_vma=False,
    )
```

```python
import math

import jax
import jax.numpy as jnp
from jax import lax
from jax.experimental import pallas as pl
from jax.experimental.pallas import tpu as pltpu
from jax.sharding import PartitionSpec as P

LOW = -2.0
QUAD = 4
BLOCK = 128
LANES = 128
PAD = 16


def swapped(array, mask):
    length = lax.axis_size("shift")
    return lax.ppermute(array, "shift", [(i, i ^ mask) for i in range(length)])


def next_quad():
    parts, count = lax.axis_size("parts"), lax.axis_size("shift")
    pairs = []
    for part in range(parts):
        by = QUAD if part % 2 == 0 else -QUAD
        for i in range(count):
            there = i + by
            if 0 <= there < count:
                pairs.append((part * count + i, part * count + there))
            elif part ^ 1 < parts:
                pairs.append((part * count + i, (part ^ 1) * count + i))
    return pairs


def forward(array):
    return lax.ppermute(array, ("parts", "shift"), next_quad())


def backward(array):
    return lax.ppermute(array, ("parts", "shift"), [(b, a) for a, b in next_quad()])


def unit_rows(raw):
    values = raw.astype(jnp.float32)
    scale = lax.rsqrt(jnp.mean(values * values, axis=1, keepdims=True) + 1e-06) / math.sqrt(
        raw.shape[1]
    )
    return (values * scale).astype(jnp.bfloat16)


def product(rows, columns):
    return lax.dot_general(
        rows, columns, (((1,), (1,)), ((), ())), preferred_element_type=jnp.float32
    )


def ids_of(packet, valid=None):
    blocks = packet.shape[0] - PAD
    values = packet[blocks:, :LANES].astype(jnp.float32)
    if valid is not None:
        values = jnp.where(valid[0] != 0, values, -1.0)
    count = blocks // BLOCK
    return [jnp.broadcast_to(values[b : b + 1], (8, LANES)) for b in range(count)]


def shares(p, q):
    meet = jnp.logical_and(p[0] <= q[-1], q[0] <= p[-1])
    return jnp.max(jnp.where(meet, 1.0, 0.0)) > 0.0


def tile_of(sims, a, b):
    tile = sims[a * BLOCK : (a + 1) * BLOCK, b * BLOCK : (b + 1) * BLOCK]
    return tile.reshape(BLOCK // 8, 8, BLOCK)


def column_best(p, q, sims, own=False):
    pieces = []
    for b in range(len(q)):
        top = jnp.full((8, BLOCK), LOW, jnp.float32)
        for a in range(len(p)):
            tile = tile_of(sims, a, b)
            if own and a == b:
                row = lax.broadcasted_iota(jnp.int32, tile.shape, 0) * 8 + (
                    lax.broadcasted_iota(jnp.int32, tile.shape, 1)
                )
                tile = jnp.where(row == lax.broadcasted_iota(jnp.int32, tile.shape, 2), LOW, tile)
            top = jnp.maximum(top, jnp.where(p[a] == q[b], jnp.max(tile, axis=0), LOW))
        pieces.append(jnp.max(top, axis=0, keepdims=True))
    return jnp.concatenate(pieces, axis=1)


def row_best(p, q, sims):
    pieces = []
    for a in range(len(p)):
        top = jnp.full((BLOCK // 8, 8, BLOCK), LOW, jnp.float32)
        for b in range(len(q)):
            shift = jnp.where(p[a] == q[b], 0.0, -4.0)
            top = jnp.maximum(top, tile_of(sims, a, b) + shift[None])
        pieces.append(jnp.max(top.reshape(BLOCK, BLOCK).T, axis=0, keepdims=True))
    return jnp.concatenate(pieces, axis=1)


def rows_of(packet):
    return packet[: packet.shape[0] - PAD, :]


def packet_kernel(ids_hbm, own_hbm, packet, held, own_ids, sems, ids_sem):
    rows, depth = held.shape
    count = rows // BLOCK
    copies = []
    ids_copy = pltpu.make_async_copy(ids_hbm, own_ids, ids_sem)
    ids_copy.start()
    for b in range(count):
        part = pl.ds(b * BLOCK, BLOCK)
        copies.append(pltpu.make_async_copy(own_hbm.at[part], held.at[part], sems.at[b]))
        copies[b].start()
    for b in range(count):
        copies[b].wait()
        part = pl.ds(b * BLOCK, BLOCK)
        packet[part, :] = unit_rows(held[part, :])
    ids_copy.wait()
    row = lax.broadcasted_iota(jnp.int32, (PAD, depth), 0)
    ids = jnp.full((PAD, depth), -1.0, jnp.float32)
    for b in range(count):
        ids = jnp.where(row == b, own_ids[b].astype(jnp.float32), ids)
    packet[rows:, :] = ids.astype(jnp.bfloat16)


def near_kernel(own_ref, mate_ref, best):
    own, mate = ids_of(own_ref), ids_of(mate_ref)
    best[...] = column_best(own, own, product(rows_of(own_ref), rows_of(own_ref)), own=True)

    @pl.when(shares(mate, own))
    def _():
        sims = product(rows_of(mate_ref), rows_of(own_ref))
        best[...] = jnp.maximum(best[...], column_best(mate, own, sims))


def partner_kernel(own_ref, partner_ref, best_in, best):
    own, partner = ids_of(own_ref), ids_of(partner_ref)
    best[...] = best_in[...]

    @pl.when(shares(partner, own))
    def _():
        sims = product(rows_of(partner_ref), rows_of(own_ref))
        best[...] = jnp.maximum(best[...], column_best(partner, own, sims))


def first_kernel(
    valid, own_ref, mate_ref, cross_ref, back_ref, best_in, best, to_mate, back
):
    own, mate, cross = ids_of(own_ref), ids_of(mate_ref), ids_of(cross_ref)
    behind = ids_of(back_ref, valid)
    best[...] = best_in[...]
    back[...] = jnp.full_like(back, LOW)
    to_mate[...] = jnp.full_like(to_mate, LOW)
    hits = [shares(mate, behind), shares(cross, behind), shares(cross, own)]

    for row, (ids, held) in enumerate(((mate, mate_ref), (cross, cross_ref))):

        @pl.when(hits[row])
        def _(row=row, ids=ids, held=held):
            sims = product(rows_of(held), rows_of(back_ref))
            back[...] = jnp.maximum(back[...], column_best(ids, behind, sims))
            to_mate[row : row + 1, :] = row_best(ids, behind, sims)

    @pl.when(hits[2])
    def _():
        sims = product(rows_of(cross_ref), rows_of(own_ref))
        best[...] = jnp.maximum(best[...], column_best(cross, own, sims))


def second_kernel(
    valid, own_ref, partner_ref, back_ref, best_in, back_in, best, to_partner, back
):
    own, partner = ids_of(own_ref), ids_of(partner_ref)
    behind = ids_of(back_ref, valid)
    best[...] = best_in[...]
    back[...] = back_in[...]
    to_partner[...] = jnp.full_like(to_partner, LOW)
    hits = [shares(own, behind), shares(partner, behind)]

    @pl.when(hits[0])
    def _():
        sims = product(rows_of(own_ref), rows_of(back_ref))
        back[...] = jnp.maximum(back[...], column_best(own, behind, sims))
        best[...] = jnp.maximum(best[...], row_best(own, behind, sims))

    @pl.when(hits[1])
    def _():
        sims = product(rows_of(partner_ref), rows_of(back_ref))
        back[...] = jnp.maximum(back[...], column_best(partner, behind, sims))
        to_partner[...] = row_best(partner, behind, sims)


def local(embeddings, block_cluster):
    rows, depth = embeddings.shape
    count = lax.axis_size("shift")
    mine = lax.axis_index("shift")
    upward = lax.axis_index("parts") % 2 == 0
    has_quad_below = mine >= QUAD
    has_quad_above = mine + QUAD < count
    receives = jnp.where(upward, has_quad_below, has_quad_above)
    returns = jnp.where(upward, has_quad_above, has_quad_below)
    valid = receives.astype(jnp.int32).reshape(1)

    smem = pl.BlockSpec(memory_space=pltpu.SMEM)
    vmem = pl.BlockSpec(memory_space=pltpu.VMEM)
    line = jax.ShapeDtypeStruct((1, rows), jnp.float32)
    lines = jax.ShapeDtypeStruct((2, rows), jnp.float32)

    def call(kernel, products, outs, specs, inputs, scratch=(), limit=40):
        return pl.pallas_call(
            kernel,
            out_shape=outs,
            in_specs=specs + [vmem] * (len(inputs) - len(specs)),
            out_specs=(vmem,) * len(outs),
            scratch_shapes=scratch,
            compiler_params=pltpu.CompilerParams(vmem_limit_bytes=limit * 1024 * 1024),
            cost_estimate=pl.CostEstimate(
                flops=2 * products * rows * rows * depth,
                bytes_accessed=2 * rows * depth,
                transcendentals=0,
            ),
        )(*inputs)

    (packet,) = call(
        packet_kernel, 0, (jax.ShapeDtypeStruct((rows + PAD, depth), jnp.bfloat16),),
        [pl.BlockSpec(memory_space=pltpu.HBM)] * 2,
        tuple(pltpu.with_memory_space_constraint(a, pltpu.HBM) for a in (block_cluster, embeddings)),
        (
            pltpu.VMEM((rows, depth), jnp.bfloat16),
            pltpu.SMEM(block_cluster.shape, jnp.int32),
            pltpu.SemaphoreType.DMA((rows // BLOCK,)),
            pltpu.SemaphoreType.DMA,
        ),
    )
    partner = swapped(packet, 2)
    behind = forward(packet)
    mate = swapped(packet, 1)
    (best,) = call(near_kernel, 0, (line,), [], (packet, mate))
    partner, best = lax.optimization_barrier((partner, best))
    cross = swapped(partner, 1)
    (best,) = call(partner_kernel, 0, (line,), [], (packet, partner, best))
    best, to_mate, back = call(
        first_kernel, 3, (line, lines, line), [smem], (valid, packet, mate, cross, behind, best)
    )
    from_mate = swapped(to_mate, 1)
    best, to_partner, back = call(
        second_kernel, 2, (line, line, line), [smem], (valid, packet, partner, behind, best, back)
    )
    from_next = jnp.where(returns, backward(back), LOW)
    from_partner = swapped(jnp.maximum(to_partner, from_mate[1:2]), 2)
    best = jnp.maximum(jnp.maximum(best, from_next), jnp.maximum(from_mate[0:1], from_partner))
    return jnp.maximum(best.reshape(rows), -1.0)


def solution(mesh):
    return jax.shard_map(
        local,
        mesh=mesh,
        in_specs=(P(("parts", "shift"), None), P(("parts", "shift"))),
        out_specs=P(("parts", "shift")),
        check_vma=False,
    )
```

```python
import math

import jax
import jax.numpy as jnp
from jax import lax
from jax.experimental import pallas as pl
from jax.experimental.pallas import tpu as pltpu
from jax.sharding import PartitionSpec as P

LOW = -2.0
QUAD = 4
BLOCK = 128
LANES = 128
PAD = 16


def swapped(array, mask):
    length = lax.axis_size("shift")
    return lax.ppermute(array, "shift", [(i, i ^ mask) for i in range(length)])


def next_quad():
    parts, count = lax.axis_size("parts"), lax.axis_size("shift")
    pairs = []
    for part in range(parts):
        by = QUAD if part % 2 == 0 else -QUAD
        for i in range(count):
            there = i + by
            if 0 <= there < count:
                pairs.append((part * count + i, part * count + there))
            elif part ^ 1 < parts:
                pairs.append((part * count + i, (part ^ 1) * count + i))
    return pairs


def ends():
    count, mine = lax.axis_size("shift"), lax.axis_index("shift")
    low, high = mine >= QUAD, mine + QUAD < count
    upward = lax.axis_index("parts") % 2 == 0
    return jnp.where(upward, low, high), jnp.where(upward, high, low)


def forward(array):
    return lax.ppermute(array, ("parts", "shift"), next_quad())


def backward(array):
    return lax.ppermute(array, ("parts", "shift"), [(b, a) for a, b in next_quad()])


def unit_rows(raw):
    values = raw.astype(jnp.float32)
    scale = lax.rsqrt(jnp.mean(values * values, axis=1, keepdims=True) + 1e-06) / math.sqrt(
        raw.shape[1]
    )
    return (values * scale).astype(jnp.bfloat16)


def product(rows, columns):
    return lax.dot_general(
        rows, columns, (((1,), (1,)), ((), ())), preferred_element_type=jnp.float32
    )


def ids_of(packet, behind=False):
    blocks = packet.shape[0] - PAD
    values = packet[blocks:, :LANES].astype(jnp.float32)
    if behind:
        values = jnp.where(ends()[0], values, -1.0)
    count = blocks // BLOCK
    return [jnp.broadcast_to(values[b : b + 1], (8, LANES)) for b in range(count)]


def shares(p, q):
    meet = jnp.logical_and(p[0] <= q[-1], q[0] <= p[-1])
    return jnp.max(jnp.where(meet, 1.0, 0.0)) > 0.0


def tile_of(sims, a, b):
    tile = sims[a * BLOCK : (a + 1) * BLOCK, b * BLOCK : (b + 1) * BLOCK]
    return tile.reshape(BLOCK // 8, 8, BLOCK)


def column_best(p, q, sims, own=False):
    pieces = []
    for b in range(len(q)):
        top = jnp.full((8, BLOCK), LOW, jnp.float32)
        for a in range(len(p)):
            tile = tile_of(sims, a, b)
            if own and a == b:
                row = lax.broadcasted_iota(jnp.int32, tile.shape, 0) * 8 + (
                    lax.broadcasted_iota(jnp.int32, tile.shape, 1)
                )
                tile = jnp.where(row == lax.broadcasted_iota(jnp.int32, tile.shape, 2), LOW, tile)
            top = jnp.maximum(top, jnp.where(p[a] == q[b], jnp.max(tile, axis=0), LOW))
        pieces.append(jnp.max(top, axis=0, keepdims=True))
    return jnp.concatenate(pieces, axis=1)


def row_best(p, q, sims):
    pieces = []
    for a in range(len(p)):
        top = jnp.full((BLOCK // 8, 8, BLOCK), LOW, jnp.float32)
        for b in range(len(q)):
            shift = jnp.where(p[a] == q[b], 0.0, -4.0)
            top = jnp.maximum(top, tile_of(sims, a, b) + shift[None])
        pieces.append(jnp.max(top.reshape(BLOCK, BLOCK).T, axis=0, keepdims=True))
    return jnp.concatenate(pieces, axis=1)


def rows_of(packet):
    return packet[: packet.shape[0] - PAD, :]


def packet_kernel(ids_hbm, own_hbm, packet, held, own_ids, sems, ids_sem):
    rows, depth = held.shape
    count = rows // BLOCK
    copies = []
    ids_copy = pltpu.make_async_copy(ids_hbm, own_ids, ids_sem)
    ids_copy.start()
    for b in range(count):
        part = pl.ds(b * BLOCK, BLOCK)
        copies.append(pltpu.make_async_copy(own_hbm.at[part], held.at[part], sems.at[b]))
        copies[b].start()
    for b in range(count):
        copies[b].wait()
        part = pl.ds(b * BLOCK, BLOCK)
        packet[part, :] = unit_rows(held[part, :])
    ids_copy.wait()
    row = lax.broadcasted_iota(jnp.int32, (PAD, depth), 0)
    ids = jnp.full((PAD, depth), -1.0, jnp.float32)
    for b in range(count):
        ids = jnp.where(row == b, own_ids[b].astype(jnp.float32), ids)
    packet[rows:, :] = ids.astype(jnp.bfloat16)


def near_kernel(own_ref, mate_ref, best):
    own, mate = ids_of(own_ref), ids_of(mate_ref)
    best[...] = column_best(own, own, product(rows_of(own_ref), rows_of(own_ref)), own=True)

    @pl.when(shares(mate, own))
    def _():
        sims = product(rows_of(mate_ref), rows_of(own_ref))
        best[...] = jnp.maximum(best[...], column_best(mate, own, sims))


def partner_kernel(own_ref, partner_ref, best_in, best):
    own, partner = ids_of(own_ref), ids_of(partner_ref)
    best[...] = best_in[...]

    @pl.when(shares(partner, own))
    def _():
        sims = product(rows_of(partner_ref), rows_of(own_ref))
        best[...] = jnp.maximum(best[...], column_best(partner, own, sims))


def behind_kernel(
    own_ref, mate_ref, partner_ref, behind_ref, best_in, best, to_mate, to_partner, back
):
    own, mate, partner = ids_of(own_ref), ids_of(mate_ref), ids_of(partner_ref)
    behind = ids_of(behind_ref, behind=True)
    best[...] = best_in[...]
    for out in (to_mate, to_partner, back):
        out[...] = jnp.full_like(out, LOW)
    pairs = ((mate, mate_ref, to_mate), (own, own_ref, best), (partner, partner_ref, to_partner))
    hits = [shares(ids, behind) for ids, held, out in pairs]
    for hit, (ids, held, out) in zip(hits, pairs):

        @pl.when(hit)
        def _(ids=ids, held=held, out=out):
            sims = product(rows_of(held), rows_of(behind_ref))
            back[...] = jnp.maximum(back[...], column_best(ids, behind, sims))
            out[...] = jnp.maximum(out[...], row_best(ids, behind, sims))


def cross_kernel(cross_ref, behind_ref, to_mate_in, back_in, to_mate, back):
    cross, behind = ids_of(cross_ref), ids_of(behind_ref, behind=True)
    to_mate[0:1, :] = to_mate_in[...]
    to_mate[1:2, :] = jnp.full_like(to_mate_in, LOW)
    back[...] = back_in[...]

    @pl.when(shares(cross, behind))
    def _():
        sims = product(rows_of(cross_ref), rows_of(behind_ref))
        back[...] = jnp.maximum(back[...], column_best(cross, behind, sims))
        to_mate[1:2, :] = row_best(cross, behind, sims)


def local(embeddings, block_cluster):
    rows, depth = embeddings.shape
    vmem = pl.BlockSpec(memory_space=pltpu.VMEM)
    line = jax.ShapeDtypeStruct((1, rows), jnp.float32)
    lines = jax.ShapeDtypeStruct((2, rows), jnp.float32)

    def call(kernel, products, outs, specs, inputs, scratch=(), limit=16):
        return pl.pallas_call(
            kernel,
            out_shape=outs,
            in_specs=specs + [vmem] * (len(inputs) - len(specs)),
            out_specs=(vmem,) * len(outs),
            scratch_shapes=scratch,
            compiler_params=pltpu.CompilerParams(vmem_limit_bytes=limit * 1024 * 1024),
            cost_estimate=pl.CostEstimate(
                flops=2 * products * rows * rows * depth,
                bytes_accessed=2 * rows * depth,
                transcendentals=0,
            ),
        )(*inputs)

    (packet,) = call(
        packet_kernel, 0, (jax.ShapeDtypeStruct((rows + PAD, depth), jnp.bfloat16),),
        [pl.BlockSpec(memory_space=pltpu.HBM)] * 2,
        tuple(pltpu.with_memory_space_constraint(a, pltpu.HBM) for a in (block_cluster, embeddings)),
        (
            pltpu.VMEM((rows, depth), jnp.bfloat16),
            pltpu.SMEM(block_cluster.shape, jnp.int32),
            pltpu.SemaphoreType.DMA((rows // BLOCK,)),
            pltpu.SemaphoreType.DMA,
        ),
    )
    partner = swapped(packet, 2)
    behind = forward(packet)
    mate = swapped(packet, 1)
    (best,) = call(near_kernel, 0, (line,), [], (packet, mate))
    partner, best = lax.optimization_barrier((partner, best))
    cross = swapped(partner, 1)
    (best,) = call(partner_kernel, 0, (line,), [], (packet, partner, best))
    best, to_mate, to_partner, back = call(
        behind_kernel, 3, (line,) * 4, [], (packet, mate, partner, behind, best)
    )
    to_mate, back = call(
        cross_kernel, 1, (lines, line), [], (cross, behind, to_mate, back)
    )
    from_mate = swapped(to_mate, 1)
    (best,) = call(partner_kernel, 1, (line,), [], (packet, cross, best))
    from_next = jnp.where(ends()[1], backward(back), LOW)
    from_partner = swapped(jnp.maximum(to_partner, from_mate[1:2]), 2)
    best = jnp.maximum(jnp.maximum(best, from_next), jnp.maximum(from_mate[0:1], from_partner))
    return jnp.maximum(best.reshape(rows), -1.0)


def solution(mesh):
    return jax.shard_map(
        local,
        mesh=mesh,
        in_specs=(P(("parts", "shift"), None), P(("parts", "shift"))),
        out_specs=P(("parts", "shift")),
        check_vma=False,
    )
```

```python
import functools
import math

import jax
import jax.numpy as jnp
from jax import lax
from jax.experimental import pallas as pl
from jax.experimental.pallas import tpu as pltpu
from jax.sharding import PartitionSpec as P

LOW = -2.0
QUAD = 4
BLOCK = 128
LANES = 128
PAD = 16


def swapped(array, mask):
    length = lax.axis_size("shift")
    return lax.ppermute(array, "shift", [(i, i ^ mask) for i in range(length)])


def next_quad():
    parts, count = lax.axis_size("parts"), lax.axis_size("shift")
    pairs = []
    for part in range(parts):
        by = QUAD if part % 2 == 0 else -QUAD
        for i in range(count):
            there = i + by
            if 0 <= there < count:
                pairs.append((part * count + i, part * count + there))
            elif part ^ 1 < parts:
                pairs.append((part * count + i, (part ^ 1) * count + i))
    return pairs


def ends():
    count, mine = lax.axis_size("shift"), lax.axis_index("shift")
    low, high = mine >= QUAD, mine + QUAD < count
    upward = lax.axis_index("parts") % 2 == 0
    return jnp.where(upward, low, high), jnp.where(upward, high, low)


def forward(array):
    return lax.ppermute(array, ("parts", "shift"), next_quad())


def backward(array):
    return lax.ppermute(array, ("parts", "shift"), [(b, a) for a, b in next_quad()])


def unit_rows(raw):
    values = raw.astype(jnp.float32)
    scale = lax.rsqrt(jnp.mean(values * values, axis=1, keepdims=True) + 1e-06) / math.sqrt(
        raw.shape[1]
    )
    return (values * scale).astype(jnp.bfloat16)


def product(rows, columns):
    return lax.dot_general(
        rows, columns, (((1,), (1,)), ((), ())), preferred_element_type=jnp.float32
    )


def ids_of(packet, behind=False):
    blocks = packet.shape[0] - PAD
    values = packet[blocks:, :LANES].astype(jnp.float32)
    if behind:
        values = jnp.where(ends()[0], values, -1.0)
    count = blocks // BLOCK
    return [jnp.broadcast_to(values[b : b + 1], (8, LANES)) for b in range(count)]


def shares(p, q):
    meet = jnp.logical_and(p[0] <= q[-1], q[0] <= p[-1])
    return jnp.max(jnp.where(meet, 1.0, 0.0)) > 0.0


def tile_of(sims, a, b):
    tile = sims[a * BLOCK : (a + 1) * BLOCK, b * BLOCK : (b + 1) * BLOCK]
    return tile.reshape(BLOCK // 8, 8, BLOCK)


def column_best(p, q, sims, own=False):
    pieces = []
    for b in range(len(q)):
        top = jnp.full((8, BLOCK), LOW, jnp.float32)
        for a in range(len(p)):
            tile = tile_of(sims, a, b)
            if own and a == b:
                row = lax.broadcasted_iota(jnp.int32, tile.shape, 0) * 8 + (
                    lax.broadcasted_iota(jnp.int32, tile.shape, 1)
                )
                tile = jnp.where(row == lax.broadcasted_iota(jnp.int32, tile.shape, 2), LOW, tile)
            top = jnp.maximum(top, jnp.where(p[a] == q[b], jnp.max(tile, axis=0), LOW))
        pieces.append(jnp.max(top, axis=0, keepdims=True))
    return jnp.concatenate(pieces, axis=1)


def row_best(p, q, sims):
    pieces = []
    for a in range(len(p)):
        top = jnp.full((BLOCK // 8, 8, BLOCK), LOW, jnp.float32)
        for b in range(len(q)):
            shift = jnp.where(p[a] == q[b], 0.0, -4.0)
            top = jnp.maximum(top, tile_of(sims, a, b) + shift[None])
        pieces.append(jnp.max(top.reshape(BLOCK, BLOCK).T, axis=0, keepdims=True))
    return jnp.concatenate(pieces, axis=1)


def rows_of(packet):
    return packet[: packet.shape[0] - PAD, :]


def packet_kernel(ids_hbm, own_hbm, packet, held, own_ids, sems, ids_sem):
    rows, depth = held.shape
    count = rows // BLOCK
    copies = []
    ids_copy = pltpu.make_async_copy(ids_hbm, own_ids, ids_sem)
    ids_copy.start()
    for b in range(count):
        part = pl.ds(b * BLOCK, BLOCK)
        copies.append(pltpu.make_async_copy(own_hbm.at[part], held.at[part], sems.at[b]))
        copies[b].start()
    for b in range(count):
        copies[b].wait()
        part = pl.ds(b * BLOCK, BLOCK)
        packet[part, :] = unit_rows(held[part, :])
    ids_copy.wait()
    row = lax.broadcasted_iota(jnp.int32, (PAD, depth), 0)
    ids = jnp.full((PAD, depth), -1.0, jnp.float32)
    for b in range(count):
        ids = jnp.where(row == b, own_ids[b].astype(jnp.float32), ids)
    packet[rows:, :] = ids.astype(jnp.bfloat16)


def own_kernel(own_ref, best):
    own = ids_of(own_ref)
    best[...] = column_best(own, own, product(rows_of(own_ref), rows_of(own_ref)), own=True)


def near_kernel(own_ref, *refs):
    *others, best_in, best = refs
    own = ids_of(own_ref)
    best[...] = best_in[...]
    ids = [ids_of(other) for other in others]
    hits = [shares(other, own) for other in ids]

    def add(other, held):
        sims = product(rows_of(held), rows_of(own_ref))
        best[...] = jnp.maximum(best[...], column_best(other, own, sims))

    every = functools.reduce(jnp.logical_and, hits)

    @pl.when(every)
    def _():
        for pair in zip(ids, others):
            add(*pair)

    if len(others) > 1:
        for hit, pair in zip(hits, zip(ids, others)):
            pl.when(hit & ~every)(functools.partial(add, *pair))


def behind_kernel(
    own_ref, mate_ref, partner_ref, behind_ref, best_in, best, to_mate, to_partner, back
):
    own, mate, partner = ids_of(own_ref), ids_of(mate_ref), ids_of(partner_ref)
    behind = ids_of(behind_ref, behind=True)
    best[...] = best_in[...]
    for out in (to_mate, to_partner, back):
        out[...] = jnp.full_like(out, LOW)
    pairs = ((mate, mate_ref, to_mate), (own, own_ref, best), (partner, partner_ref, to_partner))
    hits = [shares(ids, behind) for ids, held, out in pairs]

    def add(ids, held, out):
        sims = product(rows_of(held), rows_of(behind_ref))
        back[...] = jnp.maximum(back[...], column_best(ids, behind, sims))
        out[...] = jnp.maximum(out[...], row_best(ids, behind, sims))

    several = (hits[0] & hits[1]) | (hits[0] & hits[2]) | (hits[1] & hits[2])

    @pl.when(several)
    def _():
        for pair in pairs:
            add(*pair)

    for hit, pair in zip(hits, pairs):
        pl.when(hit & ~several)(functools.partial(add, *pair))


def cross_kernel(cross_ref, behind_ref, to_mate_in, back_in, to_mate, back):
    cross, behind = ids_of(cross_ref), ids_of(behind_ref, behind=True)
    to_mate[0:1, :] = to_mate_in[...]
    to_mate[1:2, :] = jnp.full_like(to_mate_in, LOW)
    back[...] = back_in[...]

    @pl.when(shares(cross, behind))
    def _():
        sims = product(rows_of(cross_ref), rows_of(behind_ref))
        back[...] = jnp.maximum(back[...], column_best(cross, behind, sims))
        to_mate[1:2, :] = row_best(cross, behind, sims)


def join_kernel(best_in, from_mate, from_partner, best):
    best[...] = jnp.maximum(jnp.maximum(best_in[...], from_mate[0:1, :]), from_partner[...])


def local(embeddings, block_cluster):
    rows, depth = embeddings.shape
    vmem = pl.BlockSpec(memory_space=pltpu.VMEM)
    line = jax.ShapeDtypeStruct((1, rows), jnp.float32)
    lines = jax.ShapeDtypeStruct((2, rows), jnp.float32)

    def call(kernel, products, outs, specs, inputs, scratch=(), limit=16):
        return pl.pallas_call(
            kernel,
            out_shape=outs,
            in_specs=specs + [vmem] * (len(inputs) - len(specs)),
            out_specs=(vmem,) * len(outs),
            scratch_shapes=scratch,
            compiler_params=pltpu.CompilerParams(vmem_limit_bytes=limit * 1024 * 1024),
            cost_estimate=pl.CostEstimate(
                flops=2 * products * rows * rows * depth,
                bytes_accessed=2 * rows * depth,
                transcendentals=0,
            ),
        )(*inputs)

    (packet,) = call(
        packet_kernel, 0, (jax.ShapeDtypeStruct((rows + PAD, depth), jnp.bfloat16),),
        [pl.BlockSpec(memory_space=pltpu.HBM)] * 2,
        tuple(pltpu.with_memory_space_constraint(a, pltpu.HBM) for a in (block_cluster, embeddings)),
        (
            pltpu.VMEM((rows, depth), jnp.bfloat16),
            pltpu.SMEM(block_cluster.shape, jnp.int32),
            pltpu.SemaphoreType.DMA((rows // BLOCK,)),
            pltpu.SemaphoreType.DMA,
        ),
    )
    partner = swapped(packet, 2)
    behind = forward(packet)
    mate = swapped(packet, 1)
    (best,) = call(own_kernel, 0, (line,), [], (packet,))
    partner, best = lax.optimization_barrier((partner, best))
    cross = swapped(partner, 1)
    (best,) = call(near_kernel, 0, (line,), [], (packet, partner, mate, best))
    best, to_mate, to_partner, back = call(
        behind_kernel, 3, (line,) * 4, [], (packet, mate, partner, behind, best)
    )
    to_mate, back = call(
        cross_kernel, 1, (lines, line), [], (cross, behind, to_mate, back)
    )
    from_mate = swapped(to_mate, 1)
    (best,) = call(near_kernel, 1, (line,), [], (packet, cross, best))
    from_mate, back, best = lax.optimization_barrier((from_mate, back, best))
    from_partner = swapped(jnp.maximum(to_partner, from_mate[1:2]), 2)
    from_next = backward(back)
    (best,) = call(join_kernel, 0, (line,), [], (best, from_mate, from_partner))
    best = jnp.maximum(best, jnp.where(ends()[1], from_next, LOW))
    return jnp.maximum(best.reshape(rows), -1.0)


def solution(mesh):
    return jax.shard_map(
        local,
        mesh=mesh,
        in_specs=(P(("parts", "shift"), None), P(("parts", "shift"))),
        out_specs=P(("parts", "shift")),
        check_vma=False,
    )
```

```python
import functools
import math

import jax
import jax.numpy as jnp
from jax import lax
from jax.experimental import pallas as pl
from jax.experimental.pallas import tpu as pltpu
from jax.sharding import PartitionSpec as P

LOW = -2.0
QUAD = 4
BLOCK = 128
LANES = 128
PAD = 16
STEP = 256


def swapped(array, mask):
    length = lax.axis_size("shift")
    return lax.ppermute(array, "shift", [(i, i ^ mask) for i in range(length)])


def next_quad():
    parts, count = lax.axis_size("parts"), lax.axis_size("shift")
    pairs = []
    for part in range(parts):
        by = QUAD if part % 2 == 0 else -QUAD
        for i in range(count):
            there = i + by
            if 0 <= there < count:
                pairs.append((part * count + i, part * count + there))
            elif part ^ 1 < parts:
                pairs.append((part * count + i, (part ^ 1) * count + i))
    return pairs


def ends():
    count, mine = lax.axis_size("shift"), lax.axis_index("shift")
    low, high = mine >= QUAD, mine + QUAD < count
    upward = lax.axis_index("parts") % 2 == 0
    return jnp.where(upward, low, high), jnp.where(upward, high, low)


def forward(array):
    return lax.ppermute(array, ("parts", "shift"), next_quad())


def backward(array):
    return lax.ppermute(array, ("parts", "shift"), [(b, a) for a, b in next_quad()])


def unit_rows(raw):
    values = raw.astype(jnp.float32)
    scale = lax.rsqrt(jnp.mean(values * values, axis=1, keepdims=True) + 1e-06) / math.sqrt(
        raw.shape[1]
    )
    return (values * scale).astype(jnp.bfloat16)


def product(rows, columns):
    return lax.dot_general(
        rows, columns, (((1,), (1,)), ((), ())), preferred_element_type=jnp.float32
    )


def ids_of(packet, behind=False):
    blocks = packet.shape[0] - PAD
    values = packet[blocks:, :LANES].astype(jnp.float32)
    if behind:
        values = jnp.where(ends()[0], values, -1.0)
    count = blocks // BLOCK
    return [jnp.broadcast_to(values[b : b + 1], (8, LANES)) for b in range(count)]


def shares(p, q):
    meet = jnp.logical_and(p[0] <= q[-1], q[0] <= p[-1])
    return jnp.max(jnp.where(meet, 1.0, 0.0)) > 0.0


def tile_of(sims, a, b):
    tile = sims[a * BLOCK : (a + 1) * BLOCK, b * BLOCK : (b + 1) * BLOCK]
    return tile.reshape(BLOCK // 8, 8, BLOCK)


def column_best(p, q, sims, own=False):
    pieces = []
    for b in range(len(q)):
        top = jnp.full((8, BLOCK), LOW, jnp.float32)
        for a in range(len(p)):
            tile = tile_of(sims, a, b)
            if own and a == b:
                row = lax.broadcasted_iota(jnp.int32, tile.shape, 0) * 8 + (
                    lax.broadcasted_iota(jnp.int32, tile.shape, 1)
                )
                tile = jnp.where(row == lax.broadcasted_iota(jnp.int32, tile.shape, 2), LOW, tile)
            top = jnp.maximum(top, jnp.where(p[a] == q[b], jnp.max(tile, axis=0), LOW))
        pieces.append(jnp.max(top, axis=0, keepdims=True))
    return jnp.concatenate(pieces, axis=1)


def row_best(p, q, sims):
    pieces = []
    for a in range(len(p)):
        top = jnp.full((BLOCK // 8, 8, BLOCK), LOW, jnp.float32)
        for b in range(len(q)):
            shift = jnp.where(p[a] == q[b], 0.0, -4.0)
            top = jnp.maximum(top, tile_of(sims, a, b) + shift[None])
        pieces.append(jnp.max(top.reshape(BLOCK, BLOCK).T, axis=0, keepdims=True))
    return jnp.concatenate(pieces, axis=1)


def rows_of(packet):
    return packet[: packet.shape[0] - PAD, :]


def packet_kernel(ids_hbm, own_hbm, packet, held, own_ids, sems, ids_sem):
    rows, depth = held.shape
    count = rows // BLOCK
    step = STEP
    pieces = rows // step
    copies = []
    ids_copy = pltpu.make_async_copy(ids_hbm, own_ids, ids_sem)
    ids_copy.start()
    for b in range(pieces):
        part = pl.ds(b * step, step)
        copies.append(pltpu.make_async_copy(own_hbm.at[part], held.at[part], sems.at[b]))
        copies[b].start()
    for b in range(pieces):
        copies[b].wait()
        part = pl.ds(b * step, step)
        packet[part, :] = unit_rows(held[part, :])
    ids_copy.wait()
    row = lax.broadcasted_iota(jnp.int32, (PAD, depth), 0)
    ids = jnp.full((PAD, depth), -1.0, jnp.float32)
    for b in range(count):
        ids = jnp.where(row == b, own_ids[b].astype(jnp.float32), ids)
    packet[rows:, :] = ids.astype(jnp.bfloat16)


def own_kernel(own_ref, best):
    own = ids_of(own_ref)
    best[...] = column_best(own, own, product(rows_of(own_ref), rows_of(own_ref)), own=True)


def near_kernel(own_ref, *refs):
    *others, best_in, best = refs
    own = ids_of(own_ref)
    best[...] = best_in[...]
    ids = [ids_of(other) for other in others]
    hits = [shares(other, own) for other in ids]

    def add(other, held):
        sims = product(rows_of(held), rows_of(own_ref))
        best[...] = jnp.maximum(best[...], column_best(other, own, sims))

    every = functools.reduce(jnp.logical_and, hits)

    @pl.when(every)
    def _():
        for pair in zip(ids, others):
            add(*pair)

    if len(others) > 1:
        for hit, pair in zip(hits, zip(ids, others)):
            pl.when(hit & ~every)(functools.partial(add, *pair))


def behind_kernel(
    own_ref, mate_ref, partner_ref, behind_ref, best_in, best, to_mate, to_partner, back
):
    own, mate, partner = ids_of(own_ref), ids_of(mate_ref), ids_of(partner_ref)
    behind = ids_of(behind_ref, behind=True)
    best[...] = best_in[...]
    for out in (to_mate, to_partner, back):
        out[...] = jnp.full_like(out, LOW)
    pairs = ((mate, mate_ref, to_mate), (own, own_ref, best), (partner, partner_ref, to_partner))
    hits = [shares(ids, behind) for ids, held, out in pairs]

    def add(ids, held, out):
        sims = product(rows_of(held), rows_of(behind_ref))
        back[...] = jnp.maximum(back[...], column_best(ids, behind, sims))
        out[...] = jnp.maximum(out[...], row_best(ids, behind, sims))

    several = (hits[0] & hits[1]) | (hits[0] & hits[2]) | (hits[1] & hits[2])

    @pl.when(several)
    def _():
        for pair in pairs:
            add(*pair)

    for hit, pair in zip(hits, pairs):
        pl.when(hit & ~several)(functools.partial(add, *pair))


def cross_kernel(cross_ref, behind_ref, back_in, to_cross, back):
    cross, behind = ids_of(cross_ref), ids_of(behind_ref, behind=True)
    to_cross[...] = jnp.full_like(to_cross, LOW)
    back[...] = back_in[...]

    @pl.when(shares(cross, behind))
    def _():
        sims = product(rows_of(cross_ref), rows_of(behind_ref))
        back[...] = jnp.maximum(back[...], column_best(cross, behind, sims))
        to_cross[...] = row_best(cross, behind, sims)


def join_kernel(*refs):
    *lines, best = refs
    best[...] = jnp.maximum(functools.reduce(jnp.maximum, [line[...] for line in lines]), -1.0)


def local(embeddings, block_cluster):
    rows, depth = embeddings.shape
    vmem = pl.BlockSpec(memory_space=pltpu.VMEM)
    line = jax.ShapeDtypeStruct((1, rows), jnp.float32)

    def call(kernel, products, outs, specs, inputs, scratch=(), limit=16):
        return pl.pallas_call(
            kernel,
            out_shape=outs,
            in_specs=specs + [vmem] * (len(inputs) - len(specs)),
            out_specs=(vmem,) * len(outs),
            scratch_shapes=scratch,
            compiler_params=pltpu.CompilerParams(vmem_limit_bytes=limit * 1024 * 1024),
            cost_estimate=pl.CostEstimate(
                flops=2 * products * rows * rows * depth,
                bytes_accessed=2 * rows * depth,
                transcendentals=0,
            ),
        )(*inputs)

    (packet,) = call(
        packet_kernel, 0, (jax.ShapeDtypeStruct((rows + PAD, depth), jnp.bfloat16),),
        [pl.BlockSpec(memory_space=pltpu.HBM)] * 2,
        tuple(pltpu.with_memory_space_constraint(a, pltpu.HBM) for a in (block_cluster, embeddings)),
        (
            pltpu.VMEM((rows, depth), jnp.bfloat16),
            pltpu.SMEM(block_cluster.shape, jnp.int32),
            pltpu.SemaphoreType.DMA((rows // STEP,)),
            pltpu.SemaphoreType.DMA,
        ),
    )
    partner = swapped(packet, 2)
    behind = forward(packet)
    mate = swapped(packet, 1)
    (best,) = call(own_kernel, 0, (line,), [], (packet,))
    partner, best = lax.optimization_barrier((partner, best))
    cross = swapped(partner, 1)
    (best,) = call(near_kernel, 0, (line,), [], (packet, partner, mate, best))
    best, to_mate, to_partner, back = call(
        behind_kernel, 3, (line,) * 4, [], (packet, mate, partner, behind, best)
    )
    to_cross, back = call(cross_kernel, 1, (line, line), [], (cross, behind, back))
    from_next = backward(back)
    if lax.axis_size("parts") % 2:
        from_next = jnp.where(ends()[1], from_next, LOW)
    returned = (swapped(to_cross, 3), swapped(to_partner, 2), swapped(to_mate, 1), from_next)
    (best,) = call(near_kernel, 1, (line,), [], (packet, cross, best))
    (best,) = call(join_kernel, 0, (line,), [], (best, *returned))
    return best.reshape(rows)


def solution(mesh):
    return jax.shard_map(
        local,
        mesh=mesh,
        in_specs=(P(("parts", "shift"), None), P(("parts", "shift"))),
        out_specs=P(("parts", "shift")),
        check_vma=False,
    )
```

```python
import functools
import math

import jax
import jax.numpy as jnp
from jax import lax
from jax.experimental import pallas as pl
from jax.experimental.pallas import tpu as pltpu
from jax.sharding import PartitionSpec as P

LOW = -2.0
QUAD = 4
BLOCK = 128
LANES = 128
PAD = 16
STEP = 256


def swapped(array, mask):
    length = lax.axis_size("shift")
    return lax.ppermute(array, "shift", [(i, i ^ mask) for i in range(length)])


def next_quad():
    parts, count = lax.axis_size("parts"), lax.axis_size("shift")
    pairs = []
    for part in range(parts):
        by = QUAD if part % 2 == 0 else -QUAD
        for i in range(count):
            there = i + by
            if 0 <= there < count:
                pairs.append((part * count + i, part * count + there))
            elif part ^ 1 < parts:
                pairs.append((part * count + i, (part ^ 1) * count + i))
    return pairs


def ends():
    count, mine = lax.axis_size("shift"), lax.axis_index("shift")
    low, high = mine >= QUAD, mine + QUAD < count
    upward = lax.axis_index("parts") % 2 == 0
    return jnp.where(upward, low, high), jnp.where(upward, high, low)


def forward(array):
    return lax.ppermute(array, ("parts", "shift"), next_quad())


def backward(array):
    return lax.ppermute(array, ("parts", "shift"), [(b, a) for a, b in next_quad()])


def unit_rows(raw):
    values = raw.astype(jnp.float32)
    scale = lax.rsqrt(jnp.mean(values * values, axis=1, keepdims=True) + 1e-06) / math.sqrt(
        raw.shape[1]
    )
    return (values * scale).astype(jnp.bfloat16)


def product(rows, columns):
    return lax.dot_general(
        rows, columns, (((1,), (1,)), ((), ())), preferred_element_type=jnp.float32
    )


def ids_of(packet, behind=False):
    blocks = packet.shape[0] - PAD
    values = packet[blocks:, :LANES].astype(jnp.float32)
    if behind:
        values = jnp.where(ends()[0], values, -1.0)
    count = blocks // BLOCK
    return [jnp.broadcast_to(values[b : b + 1], (8, LANES)) for b in range(count)]


def shares(p, q):
    meet = jnp.logical_and(p[0] <= q[-1], q[0] <= p[-1])
    return jnp.max(jnp.where(meet, 1.0, 0.0)) > 0.0


def tile_of(sims, a, b):
    tile = sims[a * BLOCK : (a + 1) * BLOCK, b * BLOCK : (b + 1) * BLOCK]
    return tile.reshape(BLOCK // 8, 8, BLOCK)


def column_best(p, q, sims, own=False):
    pieces = []
    for b in range(len(q)):
        top = jnp.full((8, BLOCK), LOW, jnp.float32)
        for a in range(len(p)):
            tile = tile_of(sims, a, b)
            if own and a == b:
                row = lax.broadcasted_iota(jnp.int32, tile.shape, 0) * 8 + (
                    lax.broadcasted_iota(jnp.int32, tile.shape, 1)
                )
                tile = jnp.where(row == lax.broadcasted_iota(jnp.int32, tile.shape, 2), LOW, tile)
            top = jnp.maximum(top, jnp.where(p[a] == q[b], jnp.max(tile, axis=0), LOW))
        pieces.append(jnp.max(top, axis=0, keepdims=True))
    return jnp.concatenate(pieces, axis=1)


def row_best(p, q, sims):
    pieces = []
    for a in range(len(p)):
        top = jnp.full((BLOCK // 8, 8, BLOCK), LOW, jnp.float32)
        for b in range(len(q)):
            shift = jnp.where(p[a] == q[b], 0.0, -4.0)
            top = jnp.maximum(top, tile_of(sims, a, b) + shift[None])
        pieces.append(jnp.max(top.reshape(BLOCK, BLOCK).T, axis=0, keepdims=True))
    return jnp.concatenate(pieces, axis=1)


def rows_of(packet):
    return packet[: packet.shape[0] - PAD, :]


def packet_kernel(ids_hbm, own_hbm, packet, held, own_ids, sems, ids_sem):
    rows, depth = held.shape
    count = rows // BLOCK
    step = STEP
    pieces = rows // step
    copies = []
    ids_copy = pltpu.make_async_copy(ids_hbm, own_ids, ids_sem)
    ids_copy.start()
    for b in range(pieces):
        part = pl.ds(b * step, step)
        copies.append(pltpu.make_async_copy(own_hbm.at[part], held.at[part], sems.at[b]))
        copies[b].start()
    for b in range(pieces):
        copies[b].wait()
        part = pl.ds(b * step, step)
        packet[part, :] = unit_rows(held[part, :])
    ids_copy.wait()
    row = lax.broadcasted_iota(jnp.int32, (PAD, depth), 0)
    ids = jnp.full((PAD, depth), -1.0, jnp.float32)
    for b in range(count):
        ids = jnp.where(row == b, own_ids[b].astype(jnp.float32), ids)
    packet[rows:, :] = ids.astype(jnp.bfloat16)


def own_kernel(own_ref, best):
    own = ids_of(own_ref)
    best[...] = column_best(own, own, product(rows_of(own_ref), rows_of(own_ref)), own=True)


def near_kernel(own_ref, *refs):
    *others, best_in, best = refs
    own = ids_of(own_ref)
    best[...] = best_in[...]
    ids = [ids_of(other) for other in others]
    hits = [shares(other, own) for other in ids]

    def add(other, held):
        sims = product(rows_of(held), rows_of(own_ref))
        best[...] = jnp.maximum(best[...], column_best(other, own, sims))

    every = functools.reduce(jnp.logical_and, hits)

    @pl.when(every)
    def _():
        for pair in zip(ids, others):
            add(*pair)

    if len(others) > 1:
        for hit, pair in zip(hits, zip(ids, others)):
            pl.when(hit & ~every)(functools.partial(add, *pair))


def behind_kernel(
    own_ref, mate_ref, partner_ref, behind_ref, best_in, best, to_mate, to_partner, back
):
    own, mate, partner = ids_of(own_ref), ids_of(mate_ref), ids_of(partner_ref)
    behind = ids_of(behind_ref, behind=True)
    best[...] = best_in[...]
    for out in (to_mate, to_partner, back):
        out[...] = jnp.full_like(out, LOW)
    pairs = ((mate, mate_ref, to_mate), (own, own_ref, best), (partner, partner_ref, to_partner))
    hits = [shares(ids, behind) for ids, held, out in pairs]

    def add(ids, held, out):
        sims = product(rows_of(held), rows_of(behind_ref))
        back[...] = jnp.maximum(back[...], column_best(ids, behind, sims))
        out[...] = jnp.maximum(out[...], row_best(ids, behind, sims))

    several = (hits[0] & hits[1]) | (hits[0] & hits[2]) | (hits[1] & hits[2])

    @pl.when(several)
    def _():
        for pair in pairs:
            add(*pair)

    for hit, pair in zip(hits, pairs):
        pl.when(hit & ~several)(functools.partial(add, *pair))


def cross_kernel(cross_ref, behind_ref, to_partner_in, back_in, to_chip, back):
    cross, behind = ids_of(cross_ref), ids_of(behind_ref, behind=True)
    to_chip[0:1, :] = to_partner_in[...]
    to_chip[1:2, :] = jnp.full_like(to_partner_in, LOW)
    back[...] = back_in[...]

    @pl.when(shares(cross, behind))
    def _():
        sims = product(rows_of(cross_ref), rows_of(behind_ref))
        back[...] = jnp.maximum(back[...], column_best(cross, behind, sims))
        to_chip[1:2, :] = row_best(cross, behind, sims)


def hand_on_kernel(to_mate, from_chip, out):
    out[...] = jnp.maximum(to_mate[...], from_chip[1:2, :])


def join_kernel(best_in, from_chip, from_mate, from_next, best):
    near = jnp.maximum(best_in[...], from_chip[0:1, :])
    far = jnp.maximum(from_mate[...], from_next[...])
    best[...] = jnp.maximum(jnp.maximum(near, far), -1.0)


def local(embeddings, block_cluster):
    rows, depth = embeddings.shape
    vmem = pl.BlockSpec(memory_space=pltpu.VMEM)
    line = jax.ShapeDtypeStruct((1, rows), jnp.float32)
    lines = jax.ShapeDtypeStruct((2, rows), jnp.float32)

    def call(kernel, products, outs, specs, inputs, scratch=(), limit=16):
        return pl.pallas_call(
            kernel,
            out_shape=outs,
            in_specs=specs + [vmem] * (len(inputs) - len(specs)),
            out_specs=(vmem,) * len(outs),
            scratch_shapes=scratch,
            compiler_params=pltpu.CompilerParams(vmem_limit_bytes=limit * 1024 * 1024),
            cost_estimate=pl.CostEstimate(
                flops=2 * products * rows * rows * depth,
                bytes_accessed=2 * rows * depth,
                transcendentals=0,
            ),
        )(*inputs)

    (packet,) = call(
        packet_kernel, 0, (jax.ShapeDtypeStruct((rows + PAD, depth), jnp.bfloat16),),
        [pl.BlockSpec(memory_space=pltpu.HBM)] * 2,
        tuple(pltpu.with_memory_space_constraint(a, pltpu.HBM) for a in (block_cluster, embeddings)),
        (
            pltpu.VMEM((rows, depth), jnp.bfloat16),
            pltpu.SMEM(block_cluster.shape, jnp.int32),
            pltpu.SemaphoreType.DMA((rows // STEP,)),
            pltpu.SemaphoreType.DMA,
        ),
    )
    partner = swapped(packet, 2)
    behind = forward(packet)
    mate = swapped(packet, 1)
    (best,) = call(own_kernel, 0, (line,), [], (packet,))
    partner, best = lax.optimization_barrier((partner, best))
    cross = swapped(partner, 1)
    (best,) = call(near_kernel, 0, (line,), [], (packet, partner, mate, best))
    best, to_mate, to_partner, back = call(
        behind_kernel, 3, (line,) * 4, [], (packet, mate, partner, behind, best)
    )
    to_chip, back = call(
        cross_kernel, 1, (lines, line), [], (cross, behind, to_partner, back)
    )
    from_next = backward(back)
    if lax.axis_size("parts") % 2:
        from_next = jnp.where(ends()[1], from_next, LOW)
    from_chip = swapped(to_chip, 2)
    (best,) = call(near_kernel, 1, (line,), [], (packet, cross, best))
    (to_mate,) = call(hand_on_kernel, 0, (line,), [], (to_mate, from_chip))
    from_mate = swapped(to_mate, 1)
    (best,) = call(join_kernel, 0, (line,), [], (best, from_chip, from_mate, from_next))
    return best.reshape(rows)


def solution(mesh):
    return jax.shard_map(
        local,
        mesh=mesh,
        in_specs=(P(("parts", "shift"), None), P(("parts", "shift"))),
        out_specs=P(("parts", "shift")),
        check_vma=False,
    )
```

```python
import functools
import itertools
import math

import jax
import jax.numpy as jnp
from jax import lax
from jax.experimental import pallas as pl
from jax.experimental.pallas import tpu as pltpu
from jax.sharding import PartitionSpec as P

LOW = -2.0
QUAD = 4
BLOCK = 128
LANES = 128
PAD = 16
STEP = 256


def swapped(array, mask):
    length = lax.axis_size("shift")
    return lax.ppermute(array, "shift", [(i, i ^ mask) for i in range(length)])


def next_quad():
    parts, count = lax.axis_size("parts"), lax.axis_size("shift")
    pairs = []
    for part in range(parts):
        by = QUAD if part % 2 == 0 else -QUAD
        for i in range(count):
            there = i + by
            if 0 <= there < count:
                pairs.append((part * count + i, part * count + there))
            elif part ^ 1 < parts:
                pairs.append((part * count + i, (part ^ 1) * count + i))
    return pairs


def ends():
    count, mine = lax.axis_size("shift"), lax.axis_index("shift")
    low, high = mine >= QUAD, mine + QUAD < count
    upward = lax.axis_index("parts") % 2 == 0
    return jnp.where(upward, low, high), jnp.where(upward, high, low)


def forward(array):
    return lax.ppermute(array, ("parts", "shift"), next_quad())


def backward(array):
    return lax.ppermute(array, ("parts", "shift"), [(b, a) for a, b in next_quad()])


def unit_rows(raw):
    values = raw.astype(jnp.float32)
    scale = lax.rsqrt(jnp.mean(values * values, axis=1, keepdims=True) + 1e-06) / math.sqrt(
        raw.shape[1]
    )
    return (values * scale).astype(jnp.bfloat16)


def product(rows, columns):
    return lax.dot_general(
        rows, columns, (((1,), (1,)), ((), ())), preferred_element_type=jnp.float32
    )


def ids_of(packet, behind=False):
    blocks = packet.shape[0] - PAD
    values = packet[blocks:, :LANES].astype(jnp.float32)
    if behind:
        values = jnp.where(ends()[0], values, -1.0)
    count = blocks // BLOCK
    return [jnp.broadcast_to(values[b : b + 1], (8, LANES)) for b in range(count)]


def shares(p, q):
    meet = jnp.logical_and(p[0] <= q[-1], q[0] <= p[-1])
    return jnp.max(jnp.where(meet, 1.0, 0.0)) > 0.0


def tile_of(sims, a, b):
    tile = sims[a * BLOCK : (a + 1) * BLOCK, b * BLOCK : (b + 1) * BLOCK]
    return tile.reshape(BLOCK // 8, 8, BLOCK)


def column_best(p, q, sims, own=False):
    pieces = []
    for b in range(len(q)):
        top = jnp.full((8, BLOCK), LOW, jnp.float32)
        for a in range(len(p)):
            tile = tile_of(sims, a, b)
            if own and a == b:
                row = lax.broadcasted_iota(jnp.int32, tile.shape, 0) * 8 + (
                    lax.broadcasted_iota(jnp.int32, tile.shape, 1)
                )
                tile = jnp.where(row == lax.broadcasted_iota(jnp.int32, tile.shape, 2), LOW, tile)
            top = jnp.maximum(top, jnp.where(p[a] == q[b], jnp.max(tile, axis=0), LOW))
        pieces.append(jnp.max(top, axis=0, keepdims=True))
    return jnp.concatenate(pieces, axis=1)


def row_best(p, q, sims):
    pieces = []
    for a in range(len(p)):
        top = jnp.full((BLOCK // 8, 8, BLOCK), LOW, jnp.float32)
        for b in range(len(q)):
            shift = jnp.where(p[a] == q[b], 0.0, -4.0)
            top = jnp.maximum(top, tile_of(sims, a, b) + shift[None])
        pieces.append(jnp.max(top.reshape(BLOCK, BLOCK).T, axis=0, keepdims=True))
    return jnp.concatenate(pieces, axis=1)


def rows_of(packet):
    return packet[: packet.shape[0] - PAD, :]


def packet_kernel(ids_hbm, own_hbm, packet, held, own_ids, sems, ids_sem):
    rows, depth = held.shape
    count = rows // BLOCK
    step = STEP
    pieces = rows // step
    copies = []
    ids_copy = pltpu.make_async_copy(ids_hbm, own_ids, ids_sem)
    ids_copy.start()
    for b in range(pieces):
        part = pl.ds(b * step, step)
        copies.append(pltpu.make_async_copy(own_hbm.at[part], held.at[part], sems.at[b]))
        copies[b].start()
    for b in range(pieces):
        copies[b].wait()
        part = pl.ds(b * step, step)
        packet[part, :] = unit_rows(held[part, :])
    ids_copy.wait()
    row = lax.broadcasted_iota(jnp.int32, (PAD, depth), 0)
    ids = jnp.full((PAD, depth), -1.0, jnp.float32)
    for b in range(count):
        ids = jnp.where(row == b, own_ids[b].astype(jnp.float32), ids)
    packet[rows:, :] = ids.astype(jnp.bfloat16)


def own_kernel(own_ref, best):
    own = ids_of(own_ref)
    best[...] = column_best(own, own, product(rows_of(own_ref), rows_of(own_ref)), own=True)


def near_kernel(own_ref, *refs):
    *others, best_in, best = refs
    own = ids_of(own_ref)
    best[...] = best_in[...]
    ids = [ids_of(other) for other in others]
    hits = [shares(other, own) for other in ids]

    def add(other, held):
        sims = product(rows_of(held), rows_of(own_ref))
        best[...] = jnp.maximum(best[...], column_best(other, own, sims))

    every = functools.reduce(jnp.logical_and, hits)

    @pl.when(every)
    def _():
        for pair in zip(ids, others):
            add(*pair)

    if len(others) > 1:
        for hit, pair in zip(hits, zip(ids, others)):
            pl.when(hit & ~every)(functools.partial(add, *pair))


def behind_kernel(
    own_ref, mate_ref, partner_ref, behind_ref, best_in, best, to_mate, to_partner, back
):
    own, mate, partner = ids_of(own_ref), ids_of(mate_ref), ids_of(partner_ref)
    behind = ids_of(behind_ref, behind=True)
    best[...] = best_in[...]
    for out in (to_mate, to_partner, back):
        out[...] = jnp.full_like(out, LOW)
    pairs = ((mate, mate_ref, to_mate), (own, own_ref, best), (partner, partner_ref, to_partner))
    hits = [shares(ids, behind) for ids, held, out in pairs]

    def add(ids, held, out):
        sims = product(rows_of(held), rows_of(behind_ref))
        back[...] = jnp.maximum(back[...], column_best(ids, behind, sims))
        out[...] = jnp.maximum(out[...], row_best(ids, behind, sims))

    for due in itertools.product((False, True), repeat=len(pairs)):
        if any(due):
            exact = functools.reduce(
                jnp.logical_and, [hit if wanted else ~hit for hit, wanted in zip(hits, due)]
            )

            @pl.when(exact)
            def _(due=due):
                for wanted, pair in zip(due, pairs):
                    if wanted:
                        add(*pair)


def cross_kernel(cross_ref, behind_ref, to_partner_in, back_in, to_chip, back):
    cross, behind = ids_of(cross_ref), ids_of(behind_ref, behind=True)
    to_chip[0:1, :] = to_partner_in[...]
    to_chip[1:2, :] = jnp.full_like(to_partner_in, LOW)
    back[...] = back_in[...]

    @pl.when(shares(cross, behind))
    def _():
        sims = product(rows_of(cross_ref), rows_of(behind_ref))
        back[...] = jnp.maximum(back[...], column_best(cross, behind, sims))
        to_chip[1:2, :] = row_best(cross, behind, sims)


def hand_on_kernel(to_mate, from_chip, out):
    out[...] = jnp.maximum(to_mate[...], from_chip[1:2, :])


def join_kernel(best_in, from_chip, from_mate, from_next, best):
    near = jnp.maximum(best_in[...], from_chip[0:1, :])
    far = jnp.maximum(from_mate[...], from_next[...])
    best[...] = jnp.maximum(jnp.maximum(near, far), -1.0)


def local(embeddings, block_cluster):
    rows, depth = embeddings.shape
    vmem = pl.BlockSpec(memory_space=pltpu.VMEM)
    line = jax.ShapeDtypeStruct((1, rows), jnp.float32)
    lines = jax.ShapeDtypeStruct((2, rows), jnp.float32)

    def call(kernel, products, outs, specs, inputs, scratch=(), limit=16):
        return pl.pallas_call(
            kernel,
            out_shape=outs,
            in_specs=specs + [vmem] * (len(inputs) - len(specs)),
            out_specs=(vmem,) * len(outs),
            scratch_shapes=scratch,
            compiler_params=pltpu.CompilerParams(vmem_limit_bytes=limit * 1024 * 1024),
            cost_estimate=pl.CostEstimate(
                flops=2 * products * rows * rows * depth,
                bytes_accessed=2 * rows * depth,
                transcendentals=0,
            ),
        )(*inputs)

    (packet,) = call(
        packet_kernel, 0, (jax.ShapeDtypeStruct((rows + PAD, depth), jnp.bfloat16),),
        [pl.BlockSpec(memory_space=pltpu.HBM)] * 2,
        tuple(pltpu.with_memory_space_constraint(a, pltpu.HBM) for a in (block_cluster, embeddings)),
        (
            pltpu.VMEM((rows, depth), jnp.bfloat16),
            pltpu.SMEM(block_cluster.shape, jnp.int32),
            pltpu.SemaphoreType.DMA((rows // STEP,)),
            pltpu.SemaphoreType.DMA,
        ),
    )
    partner = swapped(packet, 2)
    behind = forward(packet)
    mate = swapped(packet, 1)
    (best,) = call(own_kernel, 0, (line,), [], (packet,))
    partner, best = lax.optimization_barrier((partner, best))
    cross = swapped(partner, 1)
    (best,) = call(near_kernel, 0, (line,), [], (packet, partner, mate, best))
    best, to_mate, to_partner, back = call(
        behind_kernel, 3, (line,) * 4, [], (packet, mate, partner, behind, best)
    )
    to_chip, back = call(
        cross_kernel, 1, (lines, line), [], (cross, behind, to_partner, back)
    )
    from_next = backward(back)
    if lax.axis_size("parts") % 2:
        from_next = jnp.where(ends()[1], from_next, LOW)
    from_chip = swapped(to_chip, 2)
    (best,) = call(near_kernel, 1, (line,), [], (packet, cross, best))
    (to_mate,) = call(hand_on_kernel, 0, (line,), [], (to_mate, from_chip))
    from_mate = swapped(to_mate, 1)
    (best,) = call(join_kernel, 0, (line,), [], (best, from_chip, from_mate, from_next))
    return best.reshape(rows)


def solution(mesh):
    return jax.shard_map(
        local,
        mesh=mesh,
        in_specs=(P(("parts", "shift"), None), P(("parts", "shift"))),
        out_specs=P(("parts", "shift")),
        check_vma=False,
    )
```
